32 devices in a mesh: row: 4 (over x, core), col: 2 (over y), depth: 4 (over z).
Axes of the slice: x: 2, y: 2, z: 4, core: 2. Of those that a mesh axis runs over, the one named last changes fastest.
Arguments:
- tokens: bfloat16 [1024, 12288], P(('row', 'col'), 'depth'), may hold values from -6 to 6
- w_qkv: bfloat16 [12288, 64, 3, 128], P('depth', ('row', 'col')), may hold values from -0.0546875 to 0.0546875
- w_out: bfloat16 [64, 128, 12288], P(('row', 'col'), None, 'depth'), may hold values from -0.125 to 0.125
- positions: int32 [1024], P('depth'), may hold values from 0 to 255, as said below
- d_output: bfloat16 [1024, 12288], P(('row', 'col'), 'depth'), may hold values from -1.5 to 1.5
Outputs:
- output: bfloat16 [1024, 12288], P(('row', 'col'), 'depth')
- d_tokens: bfloat16 [1024, 12288], P(('row', 'col'), 'depth')
- d_qkv_weight: float32 [12288, 64, 3, 128], P('depth', ('row', 'col'))
- d_out_weight: float32 [64, 128, 12288], P(('row', 'col'), None, 'depth')
The draws below stay inside these ranges and needn't reach their ends.
Inputs may be any that keep to these rules, and one draw needn't show every extreme that they name: Within each sequence of 256 tokens the positions start at 0 on its first token and either rise by one from token to token or fall back to 0 where a new document begins; in some sequence one document fills all 256 tokens.
All inputs are finite; a program needn't handle non-finite values.
Results may differ from the reference program's by a relative error of at most 0.03.
Values may be sent and summed in bfloat16 or wider, within the bound.
A program may use at most 192 MiB of HBM per device.

```python
import math
import jax
import jax.numpy as jnp
from jax import lax

D = 12288
HEADS = 64
HEAD = 128
SEQ = 256
TOKENS = 1024
N_ROW = 4
N_COL = 2


def draw_positions(key, part):
    key = jax.random.fold_in(key, 7)
    first_key, second_key = jax.random.split(key)
    sequences = TOKENS // SEQ
    boundary = jax.random.randint(first_key, (sequences, SEQ), 0, SEQ) < 3
    places = jnp.arange(SEQ, dtype=jnp.int32)[None, :]
    whole_seq = jax.random.randint(second_key, (), 0, sequences)
    rows_index = jnp.arange(sequences, dtype=jnp.int32)[:, None]
    boundary = jnp.where((rows_index == whole_seq) & (places > 0), False, boundary)
    boundary = jnp.where(places == 0, True, boundary)
    starts = jnp.where(boundary, places, 0)
    latest = lax.cummax(starts, axis=1)
    return (places - latest).reshape(TOKENS).astype(jnp.int32)


def block_scale(own_key, dims, pieces, low, top_value):
    loudness = 1.0
    for axis_at, parts in pieces:
        steps = jax.random.uniform(jax.random.fold_in(jax.random.fold_in(own_key, 6), axis_at), (parts,), jnp.float32, low / len(pieces), top_value / len(pieces))
        loudness = loudness * jnp.repeat(jnp.exp(steps), dims[axis_at] // parts).reshape((-1,) + (1,) * (len(dims) - 1 - axis_at))
    return loudness


def centred(key, dims, width, limit, shards=(), kind=jnp.bfloat16):
    level = block_scale(key, dims, shards, -0.22, 0.18) if shards else 1.0
    values = jax.random.normal(key, dims, jnp.float32) * width * level
    return jnp.minimum(jnp.maximum(values, -limit), limit).astype(kind)


def setup_inputs(seed: int = 0) -> dict:
    seeds = jax.random.split(jax.random.key(seed), 6)
    tokens = centred(seeds[0], (TOKENS, D), 1.0, 6.0, ((0, 8), (1, 4)))
    w_qkv = centred(seeds[1], (D, HEADS, 3, HEAD), D ** -0.5, 0.0546875, ((0, 4), (1, 8)))
    w_out = centred(seeds[2], (HEADS, HEAD, D), (HEADS * HEAD // 4) ** -0.5, 0.125, ((0, 8), (2, 4)))
    positions = draw_positions(jax.random.fold_in(seeds[5], 71), 0)
    d_output = centred(seeds[4], (TOKENS, D), 0.25, 1.5, ((0, 8), (1, 4)))
    return {"tokens": tokens, "w_qkv": w_qkv, "w_out": w_out, "positions": positions, "d_output": d_output}


def allowed_pairs(seq_positions):
    places = jnp.arange(seq_positions.shape[0], dtype=jnp.int32)
    earlier = places[None, :] <= places[:, None]
    inside = places[None, :] >= (places - seq_positions)[:, None]
    return earlier & inside

def forward_sequence(projected_seq, seq_positions):
    score_scale = 1.0 / math.sqrt(HEAD)
    queries = projected_seq[:, :, 0].astype(jnp.float32)
    key_rows = projected_seq[:, :, 1].astype(jnp.float32)
    value_rows = projected_seq[:, :, 2].astype(jnp.float32)
    allowed = allowed_pairs(seq_positions)
    scores = jnp.einsum('ihd,jhd->hij', queries, key_rows) * score_scale
    weights = jnp.where(allowed[None], jnp.exp(scores), jnp.float32(0.0))
    probabilities = weights / lax.optimization_barrier(jnp.sum(weights, axis=-1, keepdims=True))
    rounded = probabilities.astype(jnp.bfloat16)
    mixed_heads = jnp.einsum('hij,jhd->ihd', rounded.astype(jnp.float32), value_rows).astype(jnp.bfloat16)
    return (mixed_heads, probabilities, rounded)

def backward_sequence(projected_seq, probabilities, rounded, d_mixed):
    score_scale = 1.0 / math.sqrt(HEAD)
    queries = projected_seq[:, :, 0].astype(jnp.float32)
    key_rows = projected_seq[:, :, 1].astype(jnp.float32)
    value_rows = projected_seq[:, :, 2].astype(jnp.float32)
    grad_mixed = d_mixed.astype(jnp.float32)
    d_probs = jnp.einsum('ihd,jhd->hij', grad_mixed, value_rows)
    row_delta = lax.optimization_barrier(jnp.sum(probabilities * d_probs, axis=-1, keepdims=True))
    d_scores = (probabilities * (d_probs - row_delta) * score_scale).astype(jnp.bfloat16).astype(jnp.float32)
    grad_query = jnp.einsum('hij,jhd->ihd', d_scores, key_rows)
    grad_key = jnp.einsum('hij,ihd->jhd', d_scores, queries)
    grad_value = jnp.einsum('hij,ihd->jhd', rounded.astype(jnp.float32), grad_mixed)
    return jnp.stack([grad_query, grad_key, grad_value], axis=2).astype(jnp.bfloat16)

def grouped_sum(left, right, head_groups):
    group_width = left.shape[1] // head_groups
    lefts = left.reshape(left.shape[0], head_groups, group_width).transpose(1, 0, 2)
    rights = right.reshape(head_groups, group_width, right.shape[1])

    def add_group(running, operands):
        term = jnp.dot(operands[0], operands[1], preferred_element_type=jnp.float32).astype(jnp.bfloat16)
        term = lax.optimization_barrier(term)
        return (running + term.astype(jnp.float32), None)
    start_sum = jnp.zeros((left.shape[0], right.shape[1]), jnp.float32)
    running, _ = lax.scan(add_group, start_sum, (lefts, rights))
    return running

def reference(tokens, w_qkv, w_out, positions, d_output):
    sequences = tokens.shape[0] // SEQ
    hidden = HEADS * HEAD
    head_groups = N_ROW * N_COL
    qkv_flat = w_qkv.reshape(D, HEADS * 3 * HEAD)
    out_flat = w_out.reshape(hidden, D)
    projected = jnp.dot(tokens, qkv_flat, preferred_element_type=jnp.float32).astype(jnp.bfloat16)
    projected = projected.reshape(sequences, SEQ, HEADS, 3, HEAD)
    seq_positions = positions.reshape(sequences, SEQ)
    mixed_heads, probabilities, rounded = jax.vmap(forward_sequence)(projected, seq_positions)
    mixed_flat = mixed_heads.reshape(TOKENS, hidden)
    output = grouped_sum(mixed_flat, out_flat, head_groups).astype(jnp.bfloat16)
    d_mixed = jnp.dot(d_output, out_flat.T, preferred_element_type=jnp.float32).astype(jnp.bfloat16)
    d_out_weight = jnp.dot(mixed_flat.T, d_output, preferred_element_type=jnp.float32).reshape(HEADS, HEAD, D)
    d_projected = jax.vmap(backward_sequence)(projected, probabilities, rounded, d_mixed.reshape(sequences, SEQ, HEADS, HEAD))
    d_projected = d_projected.reshape(TOKENS, HEADS * 3 * HEAD)
    d_qkv_weight = jnp.dot(tokens.T, d_projected, preferred_element_type=jnp.float32).reshape(D, HEADS, 3, HEAD)
    d_tokens = grouped_sum(d_projected, qkv_flat.T, head_groups).astype(jnp.bfloat16)
    return (output, d_tokens, d_qkv_weight, d_out_weight)
```

```python
import functools
import math

import jax
import jax.numpy as jnp
from jax import lax
from jax.experimental import pallas as pl
from jax.experimental.pallas import tpu as pltpu
from jax.sharding import PartitionSpec as P

PIECES = 2
VMEM_LIMIT = 56 * 1024 * 1024
CONTRACT_FIRST = (((0,), (0,)), ((), ()))
CONTRACT_LAST = (((1,), (1,)), ((), ()))


def dot_f32(left, right, dims=(((1,), (0,)), ((), ()))):
    return lax.dot_general(left, right, dims, preferred_element_type=jnp.float32)


def softmax_rows(positions, queries, key_rows, score_scale):
    seq_len = queries.shape[0]
    scores = dot_f32(queries, key_rows, CONTRACT_LAST) * score_scale
    rows = lax.broadcasted_iota(jnp.int32, (seq_len, seq_len), 0)
    cols = lax.broadcasted_iota(jnp.int32, (seq_len, seq_len), 1)
    allowed = (cols <= rows) & (cols >= rows - positions)
    weights = jnp.where(allowed, jnp.exp(scores), 0.0)
    return weights / jnp.sum(weights, axis=-1, keepdims=True)


def attend_kernel(score_scale, head, positions_ref, projected_ref, mixed_ref):
    queries = projected_ref[:, :head]
    key_rows = projected_ref[:, head : 2 * head]
    value_rows = projected_ref[:, 2 * head :]
    probabilities = softmax_rows(positions_ref[...], queries, key_rows, score_scale)
    mixed_ref[...] = dot_f32(probabilities.astype(jnp.bfloat16), value_rows).astype(jnp.bfloat16)


def attend_back_kernel(score_scale, head, positions_ref, projected_ref, d_mixed_ref, grads_ref):
    queries = projected_ref[:, :head]
    key_rows = projected_ref[:, head : 2 * head]
    value_rows = projected_ref[:, 2 * head :]
    d_mixed = d_mixed_ref[...]
    probabilities = softmax_rows(positions_ref[...], queries, key_rows, score_scale)
    rounded = probabilities.astype(jnp.bfloat16)
    d_probs = dot_f32(d_mixed, value_rows, CONTRACT_LAST)
    row_delta = jnp.sum(probabilities * d_probs, axis=-1, keepdims=True)
    d_scores = (probabilities * (d_probs - row_delta) * score_scale).astype(jnp.bfloat16)
    grads_ref[:, :head] = dot_f32(d_scores, key_rows).astype(jnp.bfloat16)
    grads_ref[:, head : 2 * head] = dot_f32(d_scores, queries, CONTRACT_FIRST).astype(jnp.bfloat16)
    grads_ref[:, 2 * head :] = dot_f32(rounded, d_mixed, CONTRACT_FIRST).astype(jnp.bfloat16)


def attention_call(kernel, positions, head, heads, wide_out, *arrays):
    seq_len = positions.shape[0]
    score_scale = 1.0 / math.sqrt(head)

    def per_head(width):
        return pl.BlockSpec((seq_len, width), lambda h: (0, h))

    out_width = 3 * head if wide_out else head
    flops = (14 if wide_out else 4) * heads * seq_len * seq_len * head
    return pl.pallas_call(
        functools.partial(kernel, score_scale, head),
        grid=(heads,),
        in_specs=[pl.BlockSpec((seq_len, 1), lambda h: (0, 0))]
        + [per_head(a.shape[1] // heads) for a in arrays],
        out_specs=per_head(out_width),
        out_shape=jax.ShapeDtypeStruct((seq_len, heads * out_width), jnp.bfloat16),
        cost_estimate=pl.CostEstimate(
            flops=flops,
            bytes_accessed=8 * seq_len * heads * out_width,
            transcendentals=heads * seq_len * seq_len,
        ),
        compiler_params=pltpu.CompilerParams(vmem_limit_bytes=VMEM_LIMIT),
    )(positions.reshape(seq_len, 1), *arrays)


def qkv_weight_kernel(heads, head, tokens_ref, grads_ref, out_ref):
    block = tokens_ref.shape[1]
    left = tokens_ref[...].T
    for pair in range(heads * 3 // 2):
        term = dot_f32(left, grads_ref[:, 2 * pair * head : (2 * pair + 2) * head])
        for half in range(2):
            at_head, part = divmod(2 * pair + half, 3)
            out_ref[pl.ds(part * heads + at_head, block, stride=3 * heads), :] = term[
                :, half * head : (half + 1) * head
            ]


def qkv_weight_grad(tokens_all, grads_all, heads, head):
    count, width = tokens_all.shape
    columns = grads_all.shape[1]
    block = 256
    rows = pl.pallas_call(
        functools.partial(qkv_weight_kernel, heads, head),
        grid=(width // block,),
        in_specs=[
            pl.BlockSpec((count, block), lambda i: (0, i)),
            pl.BlockSpec((count, columns), lambda i: (0, 0)),
        ],
        out_specs=pl.BlockSpec((block * 3 * heads, head), lambda i: (i, 0)),
        out_shape=jax.ShapeDtypeStruct((width * 3 * heads, head), jnp.float32),
        cost_estimate=pl.CostEstimate(
            flops=2 * count * width * columns,
            bytes_accessed=4 * width * columns + 2 * count * (width + columns),
            transcendentals=0,
        ),
        compiler_params=pltpu.CompilerParams(vmem_limit_bytes=VMEM_LIMIT),
    )(tokens_all, grads_all)
    return rows.reshape(width, 3, heads, head).transpose(0, 2, 1, 3)


def send_on(block, size):
    return lax.ppermute(block, "depth", [(i, (i + 1) % size) for i in range(size)])


def ring_sum(partial, size):
    me = lax.axis_index("depth")

    def chunk(back):
        return lax.dynamic_index_in_dim(partial, lax.rem(me + 2 * size - back, size), 0, False)

    running = chunk(1).astype(jnp.bfloat16)
    for step in range(1, size):
        arrived = send_on(running, size).astype(jnp.float32)
        running = (arrived + chunk(1 + step)).astype(jnp.bfloat16)
    return running


def ring_gather(block, size):
    me = lax.axis_index("depth")
    out = jnp.zeros((size,) + block.shape, block.dtype)
    out = lax.dynamic_update_index_in_dim(out, block, me, 0)
    for step in range(1, size):
        block = send_on(block, size)
        out = lax.dynamic_update_index_in_dim(out, block, lax.rem(me + size - step, size), 0)
    return out


def gather_rows(local_rows):
    return lax.all_gather(local_rows, ("row", "col"), axis=0, tiled=True)


def scatter_rows(whole):
    return lax.psum_scatter(whole, ("row", "col"), scatter_dimension=0, tiled=True)


def per_device(size, tokens, w_qkv, w_out, positions, d_output):
    seq_len = positions.shape[0]
    width, heads, _, head = w_qkv.shape
    hidden = heads * head
    columns = 3 * hidden
    local_rows = tokens.shape[0]
    part_rows = local_rows // PIECES
    sharers = seq_len // local_rows
    qkv_flat = w_qkv.reshape(width, columns)
    out_flat = w_out.reshape(hidden, width)

    gathered = [
        gather_rows(tokens[p * part_rows : (p + 1) * part_rows]) for p in range(PIECES)
    ]
    pieces = []
    for piece in gathered:
        partial = dot_f32(piece, qkv_flat)
        pieces.append(ring_sum(partial.reshape(size, sharers * part_rows, columns), size))
    projected = jnp.stack([p.reshape(sharers, part_rows, columns) for p in pieces], axis=1)
    projected = projected.reshape(seq_len, columns)

    grad_all = gather_rows(d_output)
    d_mixed = dot_f32(grad_all, out_flat, CONTRACT_LAST)
    d_mixed = ring_sum(d_mixed.reshape(size, seq_len, hidden), size)

    mixed = attention_call(attend_kernel, positions, head, heads, False, projected)
    heads_all = ring_gather(mixed, size).reshape(size * seq_len, hidden)
    output = scatter_rows(dot_f32(heads_all, out_flat).astype(jnp.bfloat16))

    grads = attention_call(
        attend_back_kernel, positions, head, heads, True, projected, d_mixed
    )
    d_out_weight = dot_f32(heads_all, grad_all, CONTRACT_FIRST)

    grads = grads.reshape(sharers, PIECES, part_rows, columns)
    all_grads = []
    d_tokens = []
    for p in range(PIECES):
        piece = ring_gather(grads[:, p].reshape(sharers * part_rows, columns), size)
        piece = piece.reshape(size * sharers * part_rows, columns)
        all_grads.append(piece)
        d_tokens.append(
            scatter_rows(dot_f32(piece, qkv_flat, CONTRACT_LAST).astype(jnp.bfloat16))
        )
    d_qkv_weight = qkv_weight_grad(
        jnp.concatenate(gathered, axis=0), jnp.concatenate(all_grads, axis=0), heads, head
    )
    return (
        output,
        jnp.concatenate(d_tokens, axis=0),
        d_qkv_weight,
        d_out_weight.reshape(heads, head, width),
    )


def solution(mesh):
    return jax.shard_map(
        functools.partial(per_device, mesh.shape["depth"]),
        mesh=mesh,
        in_specs=(
            P(("row", "col"), "depth"),
            P("depth", ("row", "col"), None, None),
            P(("row", "col"), None, "depth"),
            P("depth"),
            P(("row", "col"), "depth"),
        ),
        out_specs=(
            P(("row", "col"), "depth"),
            P(("row", "col"), "depth"),
            P("depth", ("row", "col"), None, None),
            P(("row", "col"), None, "depth"),
        ),
        check_vma=False,
    )
```

```python
import functools
import math

import jax
import jax.numpy as jnp
from jax import lax
from jax.experimental import pallas as pl
from jax.experimental.pallas import tpu as pltpu
from jax.sharding import PartitionSpec as P

PIECES = 2
VMEM_LIMIT = 56 * 1024 * 1024
CONTRACT_FIRST = (((0,), (0,)), ((), ()))
CONTRACT_LAST = (((1,), (1,)), ((), ()))


def dot_f32(left, right, dims=(((1,), (0,)), ((), ()))):
    return lax.dot_general(left, right, dims, preferred_element_type=jnp.float32)


def softmax_rows(positions, queries, key_rows, score_scale):
    seq_len = queries.shape[0]
    scores = dot_f32(queries, key_rows, CONTRACT_LAST) * score_scale
    rows = lax.broadcasted_iota(jnp.int32, (seq_len, seq_len), 0)
    cols = lax.broadcasted_iota(jnp.int32, (seq_len, seq_len), 1)
    allowed = (cols <= rows) & (cols >= rows - positions)
    weights = jnp.where(allowed, jnp.exp(scores), 0.0)
    return weights / jnp.sum(weights, axis=-1, keepdims=True)


def attend_kernel(score_scale, head, positions_ref, projected_ref, mixed_ref):
    queries = projected_ref[:, :head]
    key_rows = projected_ref[:, head : 2 * head]
    value_rows = projected_ref[:, 2 * head :]
    probabilities = softmax_rows(positions_ref[...], queries, key_rows, score_scale)
    mixed_ref[...] = dot_f32(probabilities.astype(jnp.bfloat16), value_rows).astype(jnp.bfloat16)


def attend_back_kernel(score_scale, head, positions_ref, projected_ref, d_mixed_ref, grads_ref):
    queries = projected_ref[:, :head]
    key_rows = projected_ref[:, head : 2 * head]
    value_rows = projected_ref[:, 2 * head :]
    d_mixed = d_mixed_ref[...]
    probabilities = softmax_rows(positions_ref[...], queries, key_rows, score_scale)
    rounded = probabilities.astype(jnp.bfloat16)
    d_probs = dot_f32(d_mixed, value_rows, CONTRACT_LAST)
    row_delta = jnp.sum(probabilities * d_probs, axis=-1, keepdims=True)
    d_scores = (probabilities * (d_probs - row_delta) * score_scale).astype(jnp.bfloat16)
    grads_ref[:, :head] = dot_f32(d_scores, key_rows).astype(jnp.bfloat16)
    grads_ref[:, head : 2 * head] = dot_f32(d_scores, queries, CONTRACT_FIRST).astype(jnp.bfloat16)
    grads_ref[:, 2 * head :] = dot_f32(rounded, d_mixed, CONTRACT_FIRST).astype(jnp.bfloat16)


def attention_call(kernel, positions, head, heads, wide_out, *arrays):
    seq_len = positions.shape[0]
    score_scale = 1.0 / math.sqrt(head)

    def per_head(width):
        return pl.BlockSpec((seq_len, width), lambda h: (0, h))

    out_width = 3 * head if wide_out else head
    flops = (14 if wide_out else 4) * heads * seq_len * seq_len * head
    return pl.pallas_call(
        functools.partial(kernel, score_scale, head),
        grid=(heads,),
        in_specs=[pl.BlockSpec((seq_len, 1), lambda h: (0, 0))]
        + [per_head(a.shape[1] // heads) for a in arrays],
        out_specs=per_head(out_width),
        out_shape=jax.ShapeDtypeStruct((seq_len, heads * out_width), jnp.bfloat16),
        cost_estimate=pl.CostEstimate(
            flops=flops,
            bytes_accessed=8 * seq_len * heads * out_width,
            transcendentals=heads * seq_len * seq_len,
        ),
        compiler_params=pltpu.CompilerParams(vmem_limit_bytes=VMEM_LIMIT),
    )(positions.reshape(seq_len, 1), *arrays)


def qkv_weight_kernel(heads, head, *refs):
    token_refs, grad_refs, out_ref = refs[:PIECES], refs[PIECES:-1], refs[-1]
    block = out_ref.shape[0] // (3 * heads)
    lefts = [ref[...].T for ref in token_refs]
    for pair in range(heads * 3 // 2):
        at = slice(2 * pair * head, (2 * pair + 2) * head)
        term = sum(dot_f32(left, ref[:, at]) for left, ref in zip(lefts, grad_refs))
        for half in range(2):
            at_head, part = divmod(2 * pair + half, 3)
            out_ref[pl.ds(part * heads + at_head, block, stride=3 * heads), :] = term[
                :, half * head : (half + 1) * head
            ]


def qkv_weight_grad(tokens_parts, grads_parts, heads, head):
    count, width = tokens_parts[0].shape
    columns = grads_parts[0].shape[1]
    block = 256
    rows = pl.pallas_call(
        functools.partial(qkv_weight_kernel, heads, head),
        grid=(width // block,),
        in_specs=[pl.BlockSpec((count, block), lambda i: (0, i))] * PIECES
        + [pl.BlockSpec((count, columns), lambda i: (0, 0))] * PIECES,
        out_specs=pl.BlockSpec((block * 3 * heads, head), lambda i: (i, 0)),
        out_shape=jax.ShapeDtypeStruct((width * 3 * heads, head), jnp.float32),
        cost_estimate=pl.CostEstimate(
            flops=2 * PIECES * count * width * columns,
            bytes_accessed=4 * width * columns + 2 * PIECES * count * (width + columns),
            transcendentals=0,
        ),
        compiler_params=pltpu.CompilerParams(vmem_limit_bytes=VMEM_LIMIT),
    )(*tokens_parts, *grads_parts)
    return rows.reshape(width, 3, heads, head).transpose(0, 2, 1, 3)


def send_on(block, size):
    return lax.ppermute(block, "depth", [(i, (i + 1) % size) for i in range(size)])


def ring_sum(partial, size):
    me = lax.axis_index("depth")

    def chunk(back):
        return lax.dynamic_index_in_dim(partial, lax.rem(me + 2 * size - back, size), 0, False)

    running = chunk(1).astype(jnp.bfloat16)
    for step in range(1, size):
        arrived = send_on(running, size).astype(jnp.float32)
        running = (arrived + chunk(1 + step)).astype(jnp.bfloat16)
    return running


def ring_gather(block, size):
    me = lax.axis_index("depth")
    out = jnp.zeros((size,) + block.shape, block.dtype)
    out = lax.dynamic_update_index_in_dim(out, block, me, 0)
    arrivals = []
    for step in range(1, size):
        block = send_on(block, size)
        arrivals.append(block)
        out = lax.dynamic_update_index_in_dim(out, block, lax.rem(me + size - step, size), 0)
    return out, arrivals


def after(block, *earlier):
    for other in earlier:
        block = block + (other[:1, :1] * jnp.zeros((), other.dtype)).astype(block.dtype)
    return block


def gather_rows(local_rows):
    return lax.all_gather(local_rows, ("row", "col"), axis=0, tiled=True)


def scatter_rows(whole):
    return lax.psum_scatter(whole, ("row", "col"), scatter_dimension=0, tiled=True)


def swap(block, mask, group):
    return lax.ppermute(block, ("row", "col"), [(i, i ^ mask) for i in range(group)])


def gather_direct(block, group, core):
    me = lax.axis_index(("row", "col"))
    masks = [m for m in range(group) if not m & core]
    out = jnp.zeros((group,) + block.shape, block.dtype)
    from_chips = [swap(block, m, group) if m else block for m in masks]
    for mask, arrived in zip(masks, from_chips):
        out = lax.dynamic_update_index_in_dim(out, arrived, me ^ mask, 0)
        other = swap(arrived, core, group)
        out = lax.dynamic_update_index_in_dim(out, other, me ^ (mask | core), 0)
    return out.reshape(group * block.shape[0], block.shape[1]), from_chips[-1]


def scatter_direct(whole, group, core):
    me = lax.axis_index(("row", "col"))
    masks = [m for m in range(group) if not m & core]
    blocks = whole.reshape(group, whole.shape[0] // group, whole.shape[1])

    def block(mask):
        return lax.dynamic_index_in_dim(blocks, me ^ mask, 0, False)

    total = 0.0
    for mask in reversed(masks):
        arrived = swap(block(mask | core), core, group)
        chip_sum = block(mask).astype(jnp.float32) + arrived.astype(jnp.float32)
        if mask:
            chip_sum = swap(chip_sum.astype(jnp.bfloat16), mask, group).astype(jnp.float32)
        total = total + chip_sum
    return total.astype(jnp.bfloat16)


def per_device(size, group, core, tokens, w_qkv, w_out, positions, d_output):
    seq_len = positions.shape[0]
    width, heads, _, head = w_qkv.shape
    hidden = heads * head
    columns = 3 * hidden
    local_rows = tokens.shape[0]
    part_rows = local_rows // PIECES
    sharers = seq_len // local_rows
    qkv_flat = w_qkv.reshape(width, columns)
    out_flat = w_out.reshape(hidden, width)

    gathered = []
    last_arrival = None
    for p in range(PIECES):
        part = tokens[p * part_rows : (p + 1) * part_rows]
        part = part if last_arrival is None else after(part, last_arrival)
        whole, last_arrival = gather_direct(part, group, core)
        gathered.append(whole)
    pieces = []
    for piece in gathered:
        partial = dot_f32(piece, qkv_flat)
        pieces.append(ring_sum(partial.reshape(size, sharers * part_rows, columns), size))
    projected = jnp.stack([p.reshape(sharers, part_rows, columns) for p in pieces], axis=1)
    projected = projected.reshape(seq_len, columns)

    grad_all = gather_rows(after(d_output, last_arrival))
    d_mixed = dot_f32(grad_all, out_flat, CONTRACT_LAST)
    d_mixed = ring_sum(d_mixed.reshape(size, seq_len, hidden), size)

    mixed = attention_call(attend_kernel, positions, head, heads, False, projected)
    heads_all, mixed_arrivals = ring_gather(mixed, size)
    heads_all = heads_all.reshape(size * seq_len, hidden)
    output_terms = dot_f32(heads_all, out_flat).astype(jnp.bfloat16)
    output = scatter_rows(output_terms)

    grads = attention_call(
        attend_back_kernel, positions, head, heads, True, projected, after(d_mixed, mixed_arrivals[-1])
    )
    d_out_weight = dot_f32(heads_all, grad_all, CONTRACT_FIRST)

    grads = grads.reshape(sharers, PIECES, part_rows, columns)
    all_grads = []
    d_tokens = []
    arrivals = None
    for p in range(PIECES):
        own = grads[:, p].reshape(sharers * part_rows, columns)
        own = own if arrivals is None else after(own, arrivals[-2], output_terms)
        piece, arrivals = ring_gather(own, size)
        piece = piece.reshape(size * sharers * part_rows, columns)
        all_grads.append(piece)
        terms = dot_f32(piece, qkv_flat, CONTRACT_LAST).astype(jnp.bfloat16)
        terms = after(terms, d_out_weight)
        d_tokens.append(scatter_direct(terms, group, core))
    d_qkv_weight = qkv_weight_grad(gathered, all_grads, heads, head)
    return (
        output,
        jnp.concatenate(d_tokens, axis=0),
        d_qkv_weight,
        d_out_weight.reshape(heads, head, width),
    )


def solution(mesh):
    return jax.shard_map(
        functools.partial(
            per_device,
            mesh.shape["depth"],
            mesh.shape["row"] * mesh.shape["col"],
            mesh.shape["col"],
        ),
        mesh=mesh,
        in_specs=(
            P(("row", "col"), "depth"),
            P("depth", ("row", "col"), None, None),
            P(("row", "col"), None, "depth"),
            P("depth"),
            P(("row", "col"), "depth"),
        ),
        out_specs=(
            P(("row", "col"), "depth"),
            P(("row", "col"), "depth"),
            P("depth", ("row", "col"), None, None),
            P(("row", "col"), None, "depth"),
        ),
        check_vma=False,
    )
```

```python
import functools
import math

import jax
import jax.numpy as jnp
from jax import lax
from jax.experimental import pallas as pl
from jax.experimental.pallas import tpu as pltpu
from jax.sharding import PartitionSpec as P

PIECES = 2
VMEM_LIMIT = 56 * 1024 * 1024
CONTRACT_FIRST = (((0,), (0,)), ((), ()))
CONTRACT_LAST = (((1,), (1,)), ((), ()))


def dot_f32(left, right, dims=(((1,), (0,)), ((), ()))):
    return lax.dot_general(left, right, dims, preferred_element_type=jnp.float32)


def softmax_rows(positions, queries, key_rows, score_scale):
    seq_len = queries.shape[0]
    scores = dot_f32(queries, key_rows, CONTRACT_LAST) * score_scale
    rows = lax.broadcasted_iota(jnp.int32, (seq_len, seq_len), 0)
    cols = lax.broadcasted_iota(jnp.int32, (seq_len, seq_len), 1)
    allowed = (cols <= rows) & (cols >= rows - positions)
    weights = jnp.where(allowed, jnp.exp(scores), 0.0)
    return weights / jnp.sum(weights, axis=-1, keepdims=True)


def attend_kernel(score_scale, head, positions_ref, projected_ref, mixed_ref):
    queries = projected_ref[:, :head]
    key_rows = projected_ref[:, head : 2 * head]
    value_rows = projected_ref[:, 2 * head :]
    probabilities = softmax_rows(positions_ref[...], queries, key_rows, score_scale)
    mixed_ref[...] = dot_f32(probabilities.astype(jnp.bfloat16), value_rows).astype(jnp.bfloat16)


def attend_back_kernel(score_scale, head, positions_ref, projected_ref, d_mixed_ref, grads_ref):
    queries = projected_ref[:, :head]
    key_rows = projected_ref[:, head : 2 * head]
    value_rows = projected_ref[:, 2 * head :]
    d_mixed = d_mixed_ref[...]
    probabilities = softmax_rows(positions_ref[...], queries, key_rows, score_scale)
    rounded = probabilities.astype(jnp.bfloat16)
    d_probs = dot_f32(d_mixed, value_rows, CONTRACT_LAST)
    row_delta = jnp.sum(probabilities * d_probs, axis=-1, keepdims=True)
    d_scores = (probabilities * (d_probs - row_delta) * score_scale).astype(jnp.bfloat16)
    grads_ref[:, :head] = dot_f32(d_scores, key_rows).astype(jnp.bfloat16)
    grads_ref[:, head : 2 * head] = dot_f32(d_scores, queries, CONTRACT_FIRST).astype(jnp.bfloat16)
    grads_ref[:, 2 * head :] = dot_f32(rounded, d_mixed, CONTRACT_FIRST).astype(jnp.bfloat16)


def attention_call(kernel, positions, head, heads, wide_out, *arrays):
    seq_len = positions.shape[0]
    score_scale = 1.0 / math.sqrt(head)

    def per_head(width):
        return pl.BlockSpec((seq_len, width), lambda h: (0, h))

    out_width = 3 * head if wide_out else head
    flops = (14 if wide_out else 4) * heads * seq_len * seq_len * head
    return pl.pallas_call(
        functools.partial(kernel, score_scale, head),
        grid=(heads,),
        in_specs=[pl.BlockSpec((seq_len, 1), lambda h: (0, 0))]
        + [per_head(a.shape[1] // heads) for a in arrays],
        out_specs=per_head(out_width),
        out_shape=jax.ShapeDtypeStruct((seq_len, heads * out_width), jnp.bfloat16),
        cost_estimate=pl.CostEstimate(
            flops=flops,
            bytes_accessed=8 * seq_len * heads * out_width,
            transcendentals=heads * seq_len * seq_len,
        ),
        compiler_params=pltpu.CompilerParams(vmem_limit_bytes=VMEM_LIMIT),
    )(positions.reshape(seq_len, 1), *arrays)


def qkv_weight_kernel(heads, head, *refs):
    token_refs, grad_refs, out_ref = refs[:PIECES], refs[PIECES:-1], refs[-1]
    block = out_ref.shape[0] // (3 * heads)
    lefts = [ref[...].T for ref in token_refs]
    for pair in range(heads * 3 // 2):
        at = slice(2 * pair * head, (2 * pair + 2) * head)
        term = sum(dot_f32(left, ref[:, at]) for left, ref in zip(lefts, grad_refs))
        for half in range(2):
            at_head, part = divmod(2 * pair + half, 3)
            out_ref[pl.ds(part * heads + at_head, block, stride=3 * heads), :] = term[
                :, half * head : (half + 1) * head
            ]


def qkv_weight_grad(tokens_parts, grads_parts, heads, head):
    count, width = tokens_parts[0].shape
    columns = grads_parts[0].shape[1]
    block = 512
    rows = pl.pallas_call(
        functools.partial(qkv_weight_kernel, heads, head),
        grid=(width // block,),
        in_specs=[pl.BlockSpec((count, block), lambda i: (0, i))] * PIECES
        + [pl.BlockSpec((count, columns), lambda i: (0, 0))] * PIECES,
        out_specs=pl.BlockSpec((block * 3 * heads, head), lambda i: (i, 0)),
        out_shape=jax.ShapeDtypeStruct((width * 3 * heads, head), jnp.float32),
        cost_estimate=pl.CostEstimate(
            flops=2 * PIECES * count * width * columns,
            bytes_accessed=4 * width * columns + 2 * PIECES * count * (width + columns),
            transcendentals=0,
        ),
        compiler_params=pltpu.CompilerParams(vmem_limit_bytes=VMEM_LIMIT),
    )(*tokens_parts, *grads_parts)
    return rows.reshape(width, 3, heads, head).transpose(0, 2, 1, 3)


def send_on(block, size):
    return lax.ppermute(block, "depth", [(i, (i + 1) % size) for i in range(size)])


def ring_sum(partial, size, before_last=()):
    me = lax.axis_index("depth")

    def chunk(back):
        return lax.dynamic_index_in_dim(partial, lax.rem(me + 2 * size - back, size), 0, False)

    running = chunk(1).astype(jnp.bfloat16)
    sums = []
    for step in range(1, size):
        if step == size - 1:
            running = after(running, *before_last)
        arrived = send_on(running, size).astype(jnp.float32)
        running = (arrived + chunk(1 + step)).astype(jnp.bfloat16)
        sums.append(running)
    return running, sums[0]


def ring_gather(block, size):
    me = lax.axis_index("depth")
    out = jnp.zeros((size,) + block.shape, block.dtype)
    out = lax.dynamic_update_index_in_dim(out, block, me, 0)
    arrivals = []
    for step in range(1, size):
        block = send_on(block, size)
        arrivals.append(block)
        out = lax.dynamic_update_index_in_dim(out, block, lax.rem(me + size - step, size), 0)
    return out, arrivals


def after(block, *earlier):
    for other in earlier:
        block = block + (other[:1, :1] * jnp.zeros((), other.dtype)).astype(block.dtype)
    return block


def gather_rows(local_rows):
    return lax.all_gather(local_rows, ("row", "col"), axis=0, tiled=True)


def scatter_rows(whole):
    return lax.psum_scatter(whole, ("row", "col"), scatter_dimension=0, tiled=True)


def swap(block, mask, group):
    return lax.ppermute(block, ("row", "col"), [(i, i ^ mask) for i in range(group)])


def scatter_direct(whole, group, core):
    me = lax.axis_index(("row", "col"))
    masks = [m for m in range(group) if not m & core]
    blocks = whole.reshape(group, whole.shape[0] // group, whole.shape[1])

    def block(mask):
        return lax.dynamic_index_in_dim(blocks, me ^ mask, 0, False)

    total = 0.0
    for mask in reversed(masks):
        arrived = swap(block(mask | core), core, group)
        chip_sum = block(mask).astype(jnp.float32) + arrived.astype(jnp.float32)
        if mask:
            chip_sum = swap(chip_sum.astype(jnp.bfloat16), mask, group).astype(jnp.float32)
        total = total + chip_sum
    return total.astype(jnp.bfloat16)


def per_device(size, group, core, tokens, w_qkv, w_out, positions, d_output):
    seq_len = positions.shape[0]
    width, heads, _, head = w_qkv.shape
    hidden = heads * head
    columns = 3 * hidden
    local_rows = tokens.shape[0]
    part_rows = local_rows // PIECES
    sharers = seq_len // local_rows
    qkv_flat = w_qkv.reshape(width, columns)
    out_flat = w_out.reshape(hidden, width)

    gathered = [
        gather_rows(tokens[p * part_rows : (p + 1) * part_rows]) for p in range(PIECES)
    ]
    grad_all = gather_rows(after(d_output, gathered[-1]))
    d_mixed_terms = dot_f32(grad_all, out_flat, CONTRACT_LAST)

    pieces = []
    for p, piece in enumerate(gathered):
        partial = dot_f32(piece, qkv_flat).reshape(size, sharers * part_rows, columns)
        before_last = (d_mixed_terms,) if p == PIECES - 1 else ()
        pieces.append(ring_sum(partial, size, before_last)[0])
    d_mixed, d_mixed_first = ring_sum(d_mixed_terms.reshape(size, seq_len, hidden), size)

    projected = jnp.stack([p.reshape(sharers, part_rows, columns) for p in pieces], axis=1)
    projected = after(projected.reshape(seq_len, columns), d_mixed_first)

    mixed = attention_call(attend_kernel, positions, head, heads, False, projected)
    heads_all, mixed_arrivals = ring_gather(mixed, size)
    heads_all = heads_all.reshape(size * seq_len, hidden)
    grads = attention_call(
        attend_back_kernel, positions, head, heads, True, projected, after(d_mixed, mixed_arrivals[-1])
    )
    heads_all = after(heads_all, grads)
    output_terms = dot_f32(heads_all, out_flat).astype(jnp.bfloat16)
    output = scatter_rows(output_terms)
    d_out_weight = dot_f32(heads_all, grad_all, CONTRACT_FIRST)

    grads = grads.reshape(sharers, PIECES, part_rows, columns)
    all_grads = []
    d_tokens = []
    arrivals = None
    for p in range(PIECES):
        own = grads[:, p].reshape(sharers * part_rows, columns)
        own = own if arrivals is None else after(own, arrivals[-1], output_terms)
        piece, arrivals = ring_gather(own, size)
        piece = piece.reshape(size * sharers * part_rows, columns)
        all_grads.append(piece)
        terms = dot_f32(piece, qkv_flat, CONTRACT_LAST).astype(jnp.bfloat16)
        terms = after(terms, d_out_weight)
        d_tokens.append(scatter_direct(terms, group, core))
    d_qkv_weight = qkv_weight_grad(gathered, all_grads, heads, head)
    return (
        output,
        jnp.concatenate(d_tokens, axis=0),
        d_qkv_weight,
        d_out_weight.reshape(heads, head, width),
    )


def solution(mesh):
    return jax.shard_map(
        functools.partial(
            per_device,
            mesh.shape["depth"],
            mesh.shape["row"] * mesh.shape["col"],
            mesh.shape["col"],
        ),
        mesh=mesh,
        in_specs=(
            P(("row", "col"), "depth"),
            P("depth", ("row", "col"), None, None),
            P(("row", "col"), None, "depth"),
            P("depth"),
            P(("row", "col"), "depth"),
        ),
        out_specs=(
            P(("row", "col"), "depth"),
            P(("row", "col"), "depth"),
            P("depth", ("row", "col"), None, None),
            P(("row", "col"), None, "depth"),
        ),
        check_vma=False,
    )
```
